32 devices in a mesh: seq: 16 (over z, x, core), head: 2 (over y).
Axes of the slice: x: 2, y: 2, z: 4, core: 2. Of those that a mesh axis runs over, the one named last changes fastest.
Arguments:
- query: bfloat16 [18432, 3072], P(('seq', 'head')), may hold values from -6 to 6
- keys: bfloat16 [18432, 3072], P(('seq', 'head')), may hold values from -6 to 6
- values: bfloat16 [18432, 3072], P(('seq', 'head')), may hold values from -6 to 6
- windows: int32 [48, 5], P('seq'), may hold values from -1 to 47, as said below
Outputs:
- attended: bfloat16 [18432, 3072], P(('seq', 'head'))
The draws below stay inside these ranges and needn't reach their ends.
Inputs may be any that keep to these rules, and one draw needn't show every extreme that they name: `windows`: row t starts with t, then lists distinct tiles, then -1 in every remaining slot. Each listed tile other than t has a tile row within 1 of t's and lies either in t's tile-frame in t's tile column or the one beside it (tile column index within 1), or in t's tile column of the tile-frame before or after; so with s = t // 3 it lies in tile column s, s - 1, s + 1, s - 4 or s + 4.
All inputs are finite; a program needn't handle non-finite values.
Results may differ from the reference program's by a relative error of at most 0.0048.
Values may be sent and summed in bfloat16 or wider, within the bound.
A program may use at most 192 MiB of HBM per device.

```python
import jax
import jax.numpy as jnp
from jax import lax

H = 24
HD = 128
TILE = 384
ROWS = 3
TFR = 4
W = 5
COLS = 4
TILES = 48
TOKENS = 18432
CH = 3072


def base_field(key, salt):
    field = jnp.clip(jax.random.normal(jax.random.fold_in(key, salt), (TOKENS, CH), jnp.float32), -6.0, 6.0)
    return field


def draw_query(key, part):
    field = base_field(key, 1)
    return field.astype(jnp.bfloat16)


def draw_keys(key, part):
    field = base_field(key, 2)
    return field.astype(jnp.bfloat16)


def draw_windows(key, part):
    tile_ids = jnp.arange(TILES, dtype=jnp.int32)
    per_frame = COLS * ROWS
    frame = tile_ids // per_frame
    column = tile_ids // ROWS % COLS
    row = tile_ids % ROWS
    frame_step = jnp.array([0, 0, 0, 0, 0, 0, 0, 0, -1, -1, -1, 1, 1, 1], dtype=jnp.int32)
    column_step = jnp.array([-1, -1, -1, 0, 0, 1, 1, 1, 0, 0, 0, 0, 0, 0], dtype=jnp.int32)
    row_step = jnp.array([-1, 0, 1, -1, 1, -1, 0, 1, -1, 0, 1, -1, 0, 1], dtype=jnp.int32)
    near_frame = frame[:, None] + frame_step[None, :]
    near_column = column[:, None] + column_step[None, :]
    near_row = row[:, None] + row_step[None, :]
    valid = (near_frame >= 0) & (near_frame < TFR) & (near_column >= 0) & (near_column < COLS) & (near_row >= 0) & (near_row < ROWS)
    named = (near_frame * COLS + near_column) * ROWS + near_row
    noise = jax.random.randint(jax.random.fold_in(key, 3), (TILES, 14), 0, 1 << 20)
    score = jnp.where(valid, noise * 16 + jnp.arange(14, dtype=jnp.int32)[None, :], 1 << 30)
    order = jnp.argsort(score, axis=1, stable=True)[:, :W - 1]
    picked = jnp.take_along_axis(named, order, axis=1)
    usable = jnp.take_along_axis(valid, order, axis=1)
    others = jnp.where(usable, picked, -1)
    return jnp.concatenate([tile_ids[:, None], others], axis=1).astype(jnp.int32)


def shard_levels(key, shape, cuts, low, largest):
    factor_of = 1.0
    for axis_at, parts in cuts:
        heights = jax.random.uniform(jax.random.fold_in(jax.random.fold_in(key, 6), axis_at), (parts,), jnp.float32, low / len(cuts), largest / len(cuts))
        factor_of = factor_of * jnp.repeat(jnp.exp(heights), shape[axis_at] // parts).reshape((-1,) + (1,) * (len(shape) - 1 - axis_at))
    return factor_of


def centred(rng, extent, deviation, bound, split=(), held_as=jnp.bfloat16):
    factor_of = shard_levels(rng, extent, split, -0.22, 0.18) if split else 1.0
    values = jax.random.normal(rng, extent, jnp.float32) * deviation * factor_of
    return jnp.minimum(jnp.maximum(values, -bound), bound).astype(held_as)


def setup_inputs(seed: int = 0) -> dict:
    seeds = jax.random.split(jax.random.key(seed), 5)
    return {
        "query": draw_query(jax.random.fold_in(seeds[4], 71), 0),
        "keys": draw_keys(jax.random.fold_in(seeds[4], 71), 0),
        "values": centred(seeds[2], (TOKENS, CH), 1.0, 6.0, ((0, 32),)),
        "windows": draw_windows(jax.random.fold_in(seeds[4], 71), 0),
    }


def reference(query, keys, values, windows):
    q_tiles = query.reshape(TILES, TILE, H, HD)
    k_tiles = keys.reshape(TILES, TILE, H, HD)
    v_tiles = values.reshape(TILES, TILE, H, HD)
    scale = 1.0 / (HD ** 0.5)

    def one_tile(item):
        q_tile, row = item
        live = row >= 0
        safe_row = jnp.maximum(row, 0).astype(jnp.int32)
        picked_k = jnp.take(k_tiles, safe_row, axis=0).reshape(W * TILE, H, HD).astype(jnp.float32)
        picked_v = jnp.take(v_tiles, safe_row, axis=0).reshape(W * TILE, H, HD).astype(jnp.float32)
        scores = jnp.einsum("qhd,khd->hqk", q_tile.astype(jnp.float32), picked_k) * scale
        key_live = jnp.repeat(live, TILE)
        scores = jnp.where(key_live[None, None, :], scores, -jnp.inf)
        top = jnp.max(scores, axis=-1, keepdims=True)
        expo = jnp.exp(scores - top)
        total = jnp.sum(expo, axis=-1)
        weights = lax.optimization_barrier(expo.astype(jnp.bfloat16)).astype(jnp.float32)
        mixed = jnp.einsum("hqk,khd->qhd", weights, picked_v)
        return (mixed / jnp.transpose(total)[:, :, None]).astype(jnp.bfloat16)

    result = lax.map(one_tile, (q_tiles, windows))
    return result.reshape(TOKENS, CH)
```

```python
import functools
import math

import jax
import jax.numpy as jnp
from jax import lax
from jax.experimental import pallas as pl
from jax.experimental.pallas import tpu as pltpu
from jax.sharding import PartitionSpec as P

HD = 128
TFR = 4
LOG2E = 1.4426950408889634
SLABS = 5
OWN = 2
AHEAD = 2


def group_sizes(heads):
    return [2] * (heads // 2) + [1] * (heads % 2)


def kernel(cfg, q_hbm, k_hbm, v_hbm, slots, offs, out, *scratch):
    seqs, peers, per_slab, tile, tokens, block, width, sizes = cfg
    n = len(sizes)
    starts = [sum(sizes[:g]) for g in range(n)]
    heads = sum(sizes)
    k_bufs, v_bufs = scratch[:n], scratch[n : 2 * n]
    (q_buf, o_buf, ex_send, ex_recv, kv_send, kv_recv, own_sem, o_send, o_recv, o_sem) = scratch[2 * n :]
    slab = per_slab * tile
    columns = seqs // TFR
    seq = lax.axis_index("seq")
    me = lax.axis_index("head")
    column = lax.rem(seq, columns)

    sends = [
        (seq + columns, 0, seq < seqs - columns),
        (seq + 1, 1, column < columns - 1),
        (seq - 1, 3, column > 0),
        (seq - columns, 4, seq >= columns),
    ]
    comes = [seq >= columns, column > 0, None, column < columns - 1, seq < seqs - columns]
    comes = [comes[code] for _, code, _ in sends]

    barrier = pltpu.get_barrier_semaphore()
    for p in range(1, peers):
        pl.semaphore_signal(
            barrier, inc=1, device_id={"head": lax.rem(me + p, peers)}, device_id_type=pl.DeviceIdType.MESH
        )
    count = peers - 1
    for target, _, there in sends:
        @pl.when(there)
        def _(target=target):
            pl.semaphore_signal(barrier, inc=1, device_id={"seq": target}, device_id_type=pl.DeviceIdType.MESH)

        count = count + there.astype(jnp.int32)
    pl.semaphore_wait(barrier, count)

    def rows_of(owner):
        return pl.ds(pl.multiple_of(owner * tokens, 16), tokens)

    def blocks_of(owner, code):
        return pl.ds((code * peers + owner) * (tokens // block), tokens // block)

    def slab_of(code):
        return pl.ds(code * (slab // block), slab // block)

    def lanes_in(owner, g):
        return pl.ds(pl.multiple_of((owner * heads + starts[g]) * HD, HD), sizes[g] * HD)

    def lanes_of(g):
        return pl.ds(starts[g] * HD, sizes[g] * HD)

    def place(g, which, owner):
        if which == 2:
            return q_buf.at[rows_of(owner), lanes_of(g)]
        return (k_bufs, v_bufs)[which][g].at[blocks_of(owner, OWN)]

    def source(which, owner, g):
        if which == 2:
            return q_hbm.at[:, lanes_in(owner, g)]
        return (k_hbm, v_hbm)[which].at[:, :, lanes_in(owner, g)]

    def exchange(g, which, p):
        to = lax.rem(me + p, peers)
        return pltpu.make_async_remote_copy(
            src_ref=source(which, to, g),
            dst_ref=place(g, which, me),
            send_sem=ex_send.at[g, which, p - 1],
            recv_sem=ex_recv.at[g, which, p - 1],
            device_id={"head": to},
            device_id_type=pl.DeviceIdType.MESH,
        )

    def own_copy(g, which):
        return pltpu.make_async_copy(source(which, me, g), place(g, which, me), own_sem.at[g, which])

    def onward(g, which, d, owner, from_hbm):
        target, code, _ = sends[d]
        buf = (k_bufs, v_bufs)[which][g]
        src = source(which, me, g) if from_hbm else place(g, which, owner)
        return pltpu.make_async_remote_copy(
            src_ref=src,
            dst_ref=buf.at[blocks_of(owner, code)],
            send_sem=kv_send.at[g, which, d],
            recv_sem=kv_recv.at[g, which, d],
            device_id={"seq": target},
            device_id_type=pl.DeviceIdType.MESH,
        )

    def whole(g, which, d):
        target, code, _ = sends[d]
        buf = (k_bufs, v_bufs)[which][g]
        return pltpu.make_async_remote_copy(
            src_ref=buf.at[slab_of(OWN)],
            dst_ref=buf.at[slab_of(code)],
            send_sem=kv_send.at[g, which, d],
            recv_sem=kv_recv.at[g, which, d],
            device_id={"seq": target},
            device_id_type=pl.DeviceIdType.MESH,
        )

    def issue(g):
        for which in range(2):
            for p in range(1, peers):
                exchange(g, which, p).start()
            for d in (0, 3, 1, 2):
                @pl.when(sends[d][2])
                def _(d=d, which=which):
                    onward(g, which, d, me, True).start()

            own_copy(g, which).start()
        for p in range(1, peers):
            exchange(g, 2, p).start()
        own_copy(g, 2).start()

    def forward(g):
        for which in range(2):
            for p in range(1, peers):
                exchange(g, which, p).wait_recv()
                owner = lax.rem(me - p + peers, peers)
                for d in (0, 3, 1, 2):
                    @pl.when(sends[d][2])
                    def _(d=d, which=which, owner=owner):
                        onward(g, which, d, owner, False).start()

    def o_copy(g, p):
        to = lax.rem(me + p, peers)
        return pltpu.make_async_remote_copy(
            src_ref=o_buf.at[rows_of(to), lanes_of(g)],
            dst_ref=out.at[:, lanes_in(me, g)],
            send_sem=o_send.at[g, p - 1],
            recv_sem=o_recv.at[g, p - 1],
            device_id={"head": to},
            device_id_type=pl.DeviceIdType.MESH,
        )

    def o_own(g):
        return pltpu.make_async_copy(
            o_buf.at[rows_of(me), lanes_of(g)], out.at[:, lanes_in(me, g)], o_sem.at[g]
        )

    def compute(g):
        for p in range(1, peers):
            exchange(g, 2, p).wait_recv()
        for which in range(3):
            own_copy(g, which).wait()
        for d in range(4):
            @pl.when(comes[d])
            def _(d=d):
                whole(g, 0, d).wait_recv()
                whole(g, 1, d).wait_recv()

        k_buf, v_buf = k_bufs[g], v_bufs[g]

        def step(i, carry):
            t = lax.div(i, sizes[g])
            h = lax.rem(i, sizes[g])
            lane = pl.ds(pl.multiple_of(h * HD, HD), HD)
            q_rows = pl.ds(pl.multiple_of(t * tile, tile), tile)
            q_lane = pl.ds(pl.multiple_of((starts[g] + h) * HD, HD), HD)
            q = q_buf[q_rows, q_lane]
            scores, picks = [], []
            top = None

            def tile_rows(buf, at):
                parts = [buf[at + b, :, lane] for b in range(tile // block)]
                return jnp.concatenate(parts, axis=0) if len(parts) > 1 else parts[0]

            for j in range(width):
                at = slots[t, j]
                s = lax.dot_general(
                    q, tile_rows(k_buf, at), (((1,), (1,)), ((), ())), preferred_element_type=jnp.float32
                )
                best = jnp.max(s, axis=1, keepdims=True) - offs[t, j]
                top = best if top is None else jnp.maximum(top, best)
                scores.append(s)
                picks.append(at)
            total = jnp.zeros((tile, 1), jnp.float32)
            mixed = jnp.zeros((tile, HD), jnp.float32)
            factor = LOG2E / HD**0.5
            for j in range(width):
                expo = jnp.exp2((scores[j] - (top + offs[t, j])) * factor)
                total = total + jnp.sum(expo, axis=1, keepdims=True)
                mixed = mixed + jnp.dot(
                    expo.astype(jnp.bfloat16), tile_rows(v_buf, picks[j]), preferred_element_type=jnp.float32
                )
            o_buf[q_rows, q_lane] = (mixed / total).astype(jnp.bfloat16)
            return carry

        lax.fori_loop(0, per_slab * sizes[g], step, 0)
        for p in range(1, peers):
            o_copy(g, p).start()
        o_own(g).start()

    for g in range(min(AHEAD, n)):
        issue(g)
    forward(0)
    for g in range(n):
        if g + AHEAD < n:
            issue(g + AHEAD)
        if g + 1 < n:
            forward(g + 1)
        compute(g)
    for g in range(n):
        for d in range(4):
            @pl.when(sends[d][2])
            def _(g=g, d=d):
                whole(g, 0, d).wait_send()
                whole(g, 1, d).wait_send()

        for p in range(1, peers):
            for which in range(3):
                exchange(g, which, p).wait_send()
            o_copy(g, p).wait()
        o_own(g).wait()


def body(query, keys, values, windows):
    seqs, peers = lax.axis_size("seq"), lax.axis_size("head")
    tokens, channels = query.shape
    per_slab, width = windows.shape
    slab = tokens * peers
    tile = slab // per_slab
    heads = channels // HD // peers
    sizes = group_sizes(heads)
    n = len(sizes)
    block = math.gcd(tokens, tile)
    cfg = (seqs, peers, per_slab, tile, tokens, block, width, sizes)
    kv = [pltpu.VMEM((SLABS * slab // block, block, size * HD), query.dtype) for size in sizes]
    columns = seqs // TFR
    seq = lax.axis_index("seq")
    live = windows >= 0
    at = jnp.where(live, windows, seq * per_slab)
    ahead = at // per_slab - seq
    code = jnp.where(ahead == 1, 3, jnp.where(ahead > 1, 4, OWN))
    code = jnp.where(ahead == -1, 1, jnp.where(ahead < -1, 0, code))
    slots = ((code * per_slab + at % per_slab) * (tile // block)).astype(jnp.int32)
    offs = jnp.where(live, 0.0, jnp.inf).astype(jnp.float32)
    others = peers - 1
    sem = pltpu.SemaphoreType.DMA
    pairs = per_slab * width * heads * tile * tile
    return pl.pallas_call(
        functools.partial(kernel, cfg),
        out_shape=jax.ShapeDtypeStruct(query.shape, query.dtype),
        in_specs=[pl.BlockSpec(memory_space=pl.ANY)] * 3 + [pl.BlockSpec(memory_space=pltpu.SMEM)] * 2,
        out_specs=pl.BlockSpec(memory_space=pl.ANY),
        scratch_shapes=kv
        + kv
        + [
            pltpu.VMEM((slab, heads * HD), query.dtype),
            pltpu.VMEM((slab, heads * HD), query.dtype),
            sem((n, 3, others)),
            sem((n, 3, others)),
            sem((n, 2, 4)),
            sem((n, 2, 4)),
            sem((n, 3)),
            sem((n, others)),
            sem((n, others)),
            sem((n,)),
        ],
        cost_estimate=pl.CostEstimate(
            flops=4 * pairs * HD, bytes_accessed=8 * tokens * channels, transcendentals=pairs
        ),
        compiler_params=pltpu.CompilerParams(
            collective_id=0, has_side_effects=True, vmem_limit_bytes=58 * 2**20
        ),
    )(
        query,
        keys.reshape(tokens // block, block, channels),
        values.reshape(tokens // block, block, channels),
        slots,
        offs,
    )


def solution(mesh):
    return jax.shard_map(
        body,
        mesh=mesh,
        in_specs=(
            P(("seq", "head"), None),
            P(("seq", "head"), None),
            P(("seq", "head"), None),
            P("seq", None),
        ),
        out_specs=P(("seq", "head"), None),
        check_vma=False,
    )
```

```python
import functools
import math

import jax
import jax.numpy as jnp
from jax import lax
from jax.experimental import pallas as pl
from jax.experimental.pallas import tpu as pltpu
from jax.sharding import PartitionSpec as P

HD = 128
TFR = 4
LOG2E = 1.4426950408889634
SLABS = 5
OWN = 2
AHEAD = 4
NEXT = 2
DEAD = 3e38


def group_sizes(heads):
    return [1] * heads


def kernel(cfg, q_hbm, k_hbm, v_hbm, win, out, *scratch):
    seqs, peers, per_slab, tile, tokens, block, width, sizes = cfg
    n = len(sizes)
    starts = [sum(sizes[:g]) for g in range(n)]
    heads = sum(sizes)
    k_bufs, v_bufs = scratch[:n], scratch[n : 2 * n]
    (q_buf, o_buf, ex_send, ex_recv, kv_send, kv_recv, own_sem, o_send, o_recv, o_sem) = scratch[2 * n :]
    slab = per_slab * tile
    columns = seqs // TFR
    seq = lax.axis_index("seq")
    me = lax.axis_index("head")
    column = lax.rem(seq, columns)

    sends = [
        (seq + columns, 0, seq < seqs - columns),
        (seq + 1, 1, column < columns - 1),
        (seq - 1, 3, column > 0),
        (seq - columns, 4, seq >= columns),
    ]
    comes = [seq >= columns, column > 0, None, column < columns - 1, seq < seqs - columns]
    comes = [comes[code] for _, code, _ in sends]

    barrier = pltpu.get_barrier_semaphore()
    for p in range(1, peers):
        pl.semaphore_signal(
            barrier, inc=1, device_id={"head": lax.rem(me + p, peers)}, device_id_type=pl.DeviceIdType.MESH
        )
    count = peers - 1
    for target, _, there in sends:
        @pl.when(there)
        def _(target=target):
            pl.semaphore_signal(barrier, inc=1, device_id={"seq": target}, device_id_type=pl.DeviceIdType.MESH)

        count = count + there.astype(jnp.int32)
    pl.semaphore_wait(barrier, count)

    def rows_of(owner):
        return pl.ds(pl.multiple_of(owner * tokens, 16), tokens)

    def blocks_of(owner, code):
        return pl.ds((code * peers + owner) * (tokens // block), tokens // block)

    def slab_of(code):
        return pl.ds(code * (slab // block), slab // block)

    def lanes_in(owner, g):
        return pl.ds(pl.multiple_of((owner * heads + starts[g]) * HD, HD), sizes[g] * HD)

    def lanes_of(g):
        return pl.ds(starts[g] * HD, sizes[g] * HD)

    def place(g, which, owner):
        if which == 2:
            return q_buf.at[rows_of(owner), lanes_of(g)]
        return (k_bufs, v_bufs)[which][g].at[blocks_of(owner, OWN)]

    def source(which, owner, g):
        if which == 2:
            return q_hbm.at[:, lanes_in(owner, g)]
        return (k_hbm, v_hbm)[which].at[:, :, lanes_in(owner, g)]

    def exchange(g, which, p):
        to = lax.rem(me + p, peers)
        return pltpu.make_async_remote_copy(
            src_ref=source(which, to, g),
            dst_ref=place(g, which, me),
            send_sem=ex_send.at[g, which, p - 1],
            recv_sem=ex_recv.at[g, which, p - 1],
            device_id={"head": to},
            device_id_type=pl.DeviceIdType.MESH,
        )

    def own_copy(g, which):
        return pltpu.make_async_copy(source(which, me, g), place(g, which, me), own_sem.at[g, which])

    def onward(g, which, d, owner, from_hbm):
        target, code, _ = sends[d]
        buf = (k_bufs, v_bufs)[which][g]
        src = source(which, me, g) if from_hbm else place(g, which, owner)
        return pltpu.make_async_remote_copy(
            src_ref=src,
            dst_ref=buf.at[blocks_of(owner, code)],
            send_sem=kv_send.at[g, which, d],
            recv_sem=kv_recv.at[g, which, d],
            device_id={"seq": target},
            device_id_type=pl.DeviceIdType.MESH,
        )

    def whole(g, which, d):
        target, code, _ = sends[d]
        buf = (k_bufs, v_bufs)[which][g]
        return pltpu.make_async_remote_copy(
            src_ref=buf.at[slab_of(OWN)],
            dst_ref=buf.at[slab_of(code)],
            send_sem=kv_send.at[g, which, d],
            recv_sem=kv_recv.at[g, which, d],
            device_id={"seq": target},
            device_id_type=pl.DeviceIdType.MESH,
        )

    def issue(g):
        for which in range(3):
            for p in range(1, peers):
                exchange(g, which, p).start()

    def issue_own(g):
        for which in range(2):
            for d in (0, 3, 1, 2):
                @pl.when(sends[d][2])
                def _(d=d, which=which):
                    onward(g, which, d, me, True).start()

        for which in range(3):
            own_copy(g, which).start()

    def forward(g):
        for which in range(2):
            for p in range(1, peers):
                exchange(g, which, p).wait_recv()
                owner = lax.rem(me - p + peers, peers)
                for d in (0, 3, 1, 2):
                    @pl.when(sends[d][2])
                    def _(d=d, which=which, owner=owner):
                        onward(g, which, d, owner, False).start()

    def o_copy(g, p):
        to = lax.rem(me + p, peers)
        return pltpu.make_async_remote_copy(
            src_ref=o_buf.at[rows_of(to), lanes_of(g)],
            dst_ref=out.at[:, lanes_in(me, g)],
            send_sem=o_send.at[g, p - 1],
            recv_sem=o_recv.at[g, p - 1],
            device_id={"head": to},
            device_id_type=pl.DeviceIdType.MESH,
        )

    def o_own(g):
        return pltpu.make_async_copy(
            o_buf.at[rows_of(me), lanes_of(g)], out.at[:, lanes_in(me, g)], o_sem.at[g]
        )

    def compute(g):
        for p in range(1, peers):
            exchange(g, 2, p).wait_recv()
        for which in range(3):
            own_copy(g, which).wait()
        for d in range(4):
            @pl.when(comes[d])
            def _(d=d):
                whole(g, 0, d).wait_recv()
                whole(g, 1, d).wait_recv()

        k_buf, v_buf = k_bufs[g], v_bufs[g]

        def step(i, carry):
            t = lax.div(i, sizes[g])
            t = jnp.where(2 * me >= peers, t, per_slab - 1 - t)
            h = lax.rem(i, sizes[g])
            lane = pl.ds(pl.multiple_of(h * HD, HD), HD)
            q_rows = pl.ds(pl.multiple_of(t * tile, tile), tile)
            q_lane = pl.ds(pl.multiple_of((starts[g] + h) * HD, HD), HD)
            q = q_buf[q_rows, q_lane]
            scores, picks, offs = [], [], []
            top = None

            def tile_rows(buf, at):
                parts = [buf[at + b, :, lane] for b in range(tile // block)]
                return jnp.concatenate(parts, axis=0) if len(parts) > 1 else parts[0]

            for j in range(width):
                w = win[t, j]
                live = w >= 0
                key_tile = jnp.where(live, w, seq * per_slab)
                ahead = lax.div(key_tile, per_slab) - seq
                code = jnp.where(ahead == 1, 3, jnp.where(ahead > 1, 4, OWN))
                code = jnp.where(ahead == -1, 1, jnp.where(ahead < -1, 0, code))
                at = (code * per_slab + lax.rem(key_tile, per_slab)) * (tile // block)
                off = jnp.where(live, 0.0, DEAD)
                s = lax.dot_general(
                    q, tile_rows(k_buf, at), (((1,), (1,)), ((), ())), preferred_element_type=jnp.float32
                )
                best = jnp.max(s, axis=1, keepdims=True) - off
                top = best if top is None else jnp.maximum(top, best)
                scores.append(s)
                picks.append(at)
                offs.append(off)
            total = jnp.zeros((tile, 1), jnp.float32)
            mixed = jnp.zeros((tile, HD), jnp.float32)
            factor = LOG2E / HD**0.5
            for j in range(width):
                expo = jnp.exp2((scores[j] - (top + offs[j])) * factor)
                total = total + jnp.sum(expo, axis=1, keepdims=True)
                mixed = mixed + jnp.dot(
                    expo.astype(jnp.bfloat16), tile_rows(v_buf, picks[j]), preferred_element_type=jnp.float32
                )
            o_buf[q_rows, q_lane] = (mixed / total).astype(jnp.bfloat16)
            if peers == 2:
                @pl.when(i == early)
                def _():
                    o_copy(g, 1).start()

            return carry

        early = ((per_slab + 1) // 2) * sizes[g] - 1
        lax.fori_loop(0, per_slab * sizes[g], step, 0)
        if peers != 2:
            for p in range(1, peers):
                o_copy(g, p).start()
        o_own(g).start()

    for g in range(max(AHEAD, NEXT)):
        if g < min(AHEAD, n):
            issue(g)
        if g < min(NEXT, n):
            issue_own(g)
    forward(0)
    for g in range(n):
        if g + AHEAD < n:
            issue(g + AHEAD)
        if g + NEXT < n:
            issue_own(g + NEXT)
        if g + 1 < n:
            forward(g + 1)
        compute(g)
    for g in range(n):
        for d in range(4):
            @pl.when(sends[d][2])
            def _(g=g, d=d):
                whole(g, 0, d).wait_send()
                whole(g, 1, d).wait_send()

        for p in range(1, peers):
            for which in range(3):
                exchange(g, which, p).wait_send()
            o_copy(g, p).wait()
        o_own(g).wait()


def body(query, keys, values, windows):
    seqs, peers = lax.axis_size("seq"), lax.axis_size("head")
    tokens, channels = query.shape
    per_slab, width = windows.shape
    slab = tokens * peers
    tile = slab // per_slab
    heads = channels // HD // peers
    sizes = group_sizes(heads)
    n = len(sizes)
    block = math.gcd(tokens, tile)
    cfg = (seqs, peers, per_slab, tile, tokens, block, width, sizes)
    kv = [pltpu.VMEM((SLABS * slab // block, block, size * HD), query.dtype) for size in sizes]
    others = peers - 1
    sem = pltpu.SemaphoreType.DMA
    pairs = per_slab * width * heads * tile * tile
    return pl.pallas_call(
        functools.partial(kernel, cfg),
        out_shape=jax.ShapeDtypeStruct(query.shape, query.dtype),
        in_specs=[pl.BlockSpec(memory_space=pl.ANY)] * 3 + [pl.BlockSpec(memory_space=pltpu.SMEM)],
        out_specs=pl.BlockSpec(memory_space=pl.ANY),
        scratch_shapes=kv
        + kv
        + [
            pltpu.VMEM((slab, heads * HD), query.dtype),
            pltpu.VMEM((slab, heads * HD), query.dtype),
            sem((n, 3, others)),
            sem((n, 3, others)),
            sem((n, 2, 4)),
            sem((n, 2, 4)),
            sem((n, 3)),
            sem((n, others)),
            sem((n, others)),
            sem((n,)),
        ],
        cost_estimate=pl.CostEstimate(
            flops=4 * pairs * HD, bytes_accessed=8 * tokens * channels, transcendentals=pairs
        ),
        compiler_params=pltpu.CompilerParams(
            collective_id=0, has_side_effects=True, vmem_limit_bytes=58 * 2**20
        ),
    )(
        query,
        keys.reshape(tokens // block, block, channels),
        values.reshape(tokens // block, block, channels),
        windows,
    )


def solution(mesh):
    return jax.shard_map(
        body,
        mesh=mesh,
        in_specs=(
            P(("seq", "head"), None),
            P(("seq", "head"), None),
            P(("seq", "head"), None),
            P("seq", None),
        ),
        out_specs=P(("seq", "head"), None),
        check_vma=False,
    )
```

```python
import functools
import math

import jax
import jax.numpy as jnp
from jax import lax
from jax.experimental import pallas as pl
from jax.experimental.pallas import tpu as pltpu
from jax.sharding import PartitionSpec as P

HD = 128
TFR = 4
LOG2E = 1.4426950408889634
SLABS = 5
OWN = 2
AHEAD = 4
NEXT = 2
DEAD = 3e38


def group_sizes(heads):
    return [1] * heads


def kernel(cfg, q_hbm, k_hbm, v_hbm, win, out, *scratch):
    seqs, peers, per_slab, tile, tokens, block, width, sizes = cfg
    n = len(sizes)
    starts = [sum(sizes[:g]) for g in range(n)]
    heads = sum(sizes)
    k_bufs, v_bufs = scratch[:n], scratch[n : 2 * n]
    (q_buf, o_buf, ex_send, ex_recv, kv_send, kv_recv, own_sem, o_send, o_recv, o_sem) = scratch[2 * n :]
    slab = per_slab * tile
    columns = seqs // TFR
    seq = lax.axis_index("seq")
    me = lax.axis_index("head")
    column = lax.rem(seq, columns)

    sends = [
        (seq + columns, 0, seq < seqs - columns),
        (seq + 1, 1, column < columns - 1),
        (seq - 1, 3, column > 0),
        (seq - columns, 4, seq >= columns),
    ]
    comes = [seq >= columns, column > 0, None, column < columns - 1, seq < seqs - columns]
    comes = [comes[code] for _, code, _ in sends]

    barrier = pltpu.get_barrier_semaphore()
    for p in range(1, peers):
        pl.semaphore_signal(
            barrier, inc=1, device_id={"head": lax.rem(me + p, peers)}, device_id_type=pl.DeviceIdType.MESH
        )
    count = peers - 1
    for target, _, there in sends:
        @pl.when(there)
        def _(target=target):
            pl.semaphore_signal(barrier, inc=1, device_id={"seq": target}, device_id_type=pl.DeviceIdType.MESH)

        count = count + there.astype(jnp.int32)
    pl.semaphore_wait(barrier, count)

    def rows_of(owner):
        return pl.ds(pl.multiple_of(owner * tokens, 16), tokens)

    def blocks_of(owner, code):
        return pl.ds((code * peers + owner) * (tokens // block), tokens // block)

    def slab_of(code):
        return pl.ds(code * (slab // block), slab // block)

    def lanes_in(owner, g):
        return pl.ds(pl.multiple_of((owner * heads + starts[g]) * HD, HD), sizes[g] * HD)

    def lanes_of(g):
        return pl.ds(starts[g] * HD, sizes[g] * HD)

    def place(g, which, owner):
        if which == 2:
            return q_buf.at[rows_of(owner), lanes_of(g)]
        return (k_bufs, v_bufs)[which][g].at[blocks_of(owner, OWN)]

    def source(which, owner, g):
        if which == 2:
            return q_hbm.at[:, lanes_in(owner, g)]
        return (k_hbm, v_hbm)[which].at[:, :, lanes_in(owner, g)]

    def exchange(g, which, p):
        to = lax.rem(me + p, peers)
        return pltpu.make_async_remote_copy(
            src_ref=source(which, to, g),
            dst_ref=place(g, which, me),
            send_sem=ex_send.at[g, which, p - 1],
            recv_sem=ex_recv.at[g, which, p - 1],
            device_id={"head": to},
            device_id_type=pl.DeviceIdType.MESH,
        )

    def own_copy(g, which):
        return pltpu.make_async_copy(source(which, me, g), place(g, which, me), own_sem.at[g, which])

    def onward(g, which, d, owner, from_hbm):
        target, code, _ = sends[d]
        buf = (k_bufs, v_bufs)[which][g]
        src = source(which, me, g) if from_hbm else place(g, which, owner)
        return pltpu.make_async_remote_copy(
            src_ref=src,
            dst_ref=buf.at[blocks_of(owner, code)],
            send_sem=kv_send.at[g, which, d],
            recv_sem=kv_recv.at[g, which, d],
            device_id={"seq": target},
            device_id_type=pl.DeviceIdType.MESH,
        )

    def whole(g, which, d):
        target, code, _ = sends[d]
        buf = (k_bufs, v_bufs)[which][g]
        return pltpu.make_async_remote_copy(
            src_ref=buf.at[slab_of(OWN)],
            dst_ref=buf.at[slab_of(code)],
            send_sem=kv_send.at[g, which, d],
            recv_sem=kv_recv.at[g, which, d],
            device_id={"seq": target},
            device_id_type=pl.DeviceIdType.MESH,
        )

    def issue(g):
        for which in range(2):
            for p in range(1, peers):
                exchange(g, which, p).start()

    def issue_query(g):
        for p in range(1, peers):
            exchange(g, 2, p).start()

    def issue_own(g):
        for which in range(2):
            for d in (0, 3, 1, 2):
                @pl.when(sends[d][2])
                def _(d=d, which=which):
                    onward(g, which, d, me, True).start()

        for which in range(3):
            own_copy(g, which).start()

    def forward(g):
        for which in range(2):
            for p in range(1, peers):
                exchange(g, which, p).wait_recv()
                owner = lax.rem(me - p + peers, peers)
                for d in (0, 3, 1, 2):
                    @pl.when(sends[d][2])
                    def _(d=d, which=which, owner=owner):
                        onward(g, which, d, owner, False).start()

    def o_copy(g, p):
        to = lax.rem(me + p, peers)
        return pltpu.make_async_remote_copy(
            src_ref=o_buf.at[rows_of(to), lanes_of(g)],
            dst_ref=out.at[:, lanes_in(me, g)],
            send_sem=o_send.at[g, p - 1],
            recv_sem=o_recv.at[g, p - 1],
            device_id={"head": to},
            device_id_type=pl.DeviceIdType.MESH,
        )

    def o_own(g):
        return pltpu.make_async_copy(
            o_buf.at[rows_of(me), lanes_of(g)], out.at[:, lanes_in(me, g)], o_sem.at[g]
        )

    def compute(g):
        for p in range(1, peers):
            exchange(g, 2, p).wait_recv()
        for which in range(3):
            own_copy(g, which).wait()
        for d in range(4):
            @pl.when(comes[d])
            def _(d=d):
                whole(g, 0, d).wait_recv()
                whole(g, 1, d).wait_recv()

        k_buf, v_buf = k_bufs[g], v_bufs[g]

        def step(i, carry):
            t = lax.div(i, sizes[g])
            t = jnp.where(2 * me >= peers, t, per_slab - 1 - t)
            h = lax.rem(i, sizes[g])
            lane = pl.ds(pl.multiple_of(h * HD, HD), HD)
            q_rows = pl.ds(pl.multiple_of(t * tile, tile), tile)
            q_lane = pl.ds(pl.multiple_of((starts[g] + h) * HD, HD), HD)
            q = q_buf[q_rows, q_lane]
            scores, picks, offs = [], [], []
            top = None

            def tile_rows(buf, at):
                parts = [buf[at + b, :, lane] for b in range(tile // block)]
                return jnp.concatenate(parts, axis=0) if len(parts) > 1 else parts[0]

            for j in range(width):
                w = win[t, j]
                live = w >= 0
                key_tile = jnp.where(live, w, seq * per_slab)
                ahead = lax.div(key_tile, per_slab) - seq
                code = jnp.where(ahead == 1, 3, jnp.where(ahead > 1, 4, OWN))
                code = jnp.where(ahead == -1, 1, jnp.where(ahead < -1, 0, code))
                at = (code * per_slab + lax.rem(key_tile, per_slab)) * (tile // block)
                off = jnp.where(live, 0.0, DEAD)
                s = lax.dot_general(
                    q, tile_rows(k_buf, at), (((1,), (1,)), ((), ())), preferred_element_type=jnp.float32
                )
                best = jnp.max(s, axis=1, keepdims=True) - off
                top = best if top is None else jnp.maximum(top, best)
                scores.append(s)
                picks.append(at)
                offs.append(off)
            total = jnp.zeros((tile, 1), jnp.float32)
            mixed = jnp.zeros((tile, HD), jnp.float32)
            factor = LOG2E / HD**0.5
            for j in range(width):
                expo = jnp.exp2((scores[j] - (top + offs[j])) * factor)
                total = total + jnp.sum(expo, axis=1, keepdims=True)
                mixed = mixed + jnp.dot(
                    expo.astype(jnp.bfloat16), tile_rows(v_buf, picks[j]), preferred_element_type=jnp.float32
                )
            o_buf[q_rows, q_lane] = (mixed / total).astype(jnp.bfloat16)
            if peers == 2:
                @pl.when(i == early)
                def _():
                    o_copy(g, 1).start()

            return carry

        early = ((per_slab + 1) // 2) * sizes[g] - 1
        lax.fori_loop(0, per_slab * sizes[g], step, 0)
        if peers != 2:
            for p in range(1, peers):
                o_copy(g, p).start()
        o_own(g).start()

    for g in range(max(AHEAD, NEXT)):
        if g < min(AHEAD, n):
            issue(g)
        if g < min(NEXT, n):
            issue_own(g)
            issue_query(g)
    forward(0)
    for g in range(n):
        if g + AHEAD < n:
            issue(g + AHEAD)
        if g + NEXT < n:
            issue_own(g + NEXT)
            issue_query(g + NEXT)
        if g + 1 < n:
            forward(g + 1)
        compute(g)
    for g in range(n):
        for d in range(4):
            @pl.when(sends[d][2])
            def _(g=g, d=d):
                whole(g, 0, d).wait_send()
                whole(g, 1, d).wait_send()

        for p in range(1, peers):
            for which in range(3):
                exchange(g, which, p).wait_send()
            o_copy(g, p).wait()
        o_own(g).wait()


def body(query, keys, values, windows):
    seqs, peers = lax.axis_size("seq"), lax.axis_size("head")
    tokens, channels = query.shape
    per_slab, width = windows.shape
    slab = tokens * peers
    tile = slab // per_slab
    heads = channels // HD // peers
    sizes = group_sizes(heads)
    n = len(sizes)
    block = math.gcd(tokens, tile)
    cfg = (seqs, peers, per_slab, tile, tokens, block, width, sizes)
    kv = [pltpu.VMEM((SLABS * slab // block, block, size * HD), query.dtype) for size in sizes]
    others = peers - 1
    sem = pltpu.SemaphoreType.DMA
    pairs = per_slab * width * heads * tile * tile
    return pl.pallas_call(
        functools.partial(kernel, cfg),
        out_shape=jax.ShapeDtypeStruct(query.shape, query.dtype),
        in_specs=[pl.BlockSpec(memory_space=pl.ANY)] * 3 + [pl.BlockSpec(memory_space=pltpu.SMEM)],
        out_specs=pl.BlockSpec(memory_space=pl.ANY),
        scratch_shapes=kv
        + kv
        + [
            pltpu.VMEM((slab, heads * HD), query.dtype),
            pltpu.VMEM((slab, heads * HD), query.dtype),
            sem((n, 3, others)),
            sem((n, 3, others)),
            sem((n, 2, 4)),
            sem((n, 2, 4)),
            sem((n, 3)),
            sem((n, others)),
            sem((n, others)),
            sem((n,)),
        ],
        cost_estimate=pl.CostEstimate(
            flops=4 * pairs * HD, bytes_accessed=8 * tokens * channels, transcendentals=pairs
        ),
        compiler_params=pltpu.CompilerParams(
            collective_id=0, has_side_effects=True, vmem_limit_bytes=58 * 2**20
        ),
    )(
        query,
        keys.reshape(tokens // block, block, channels),
        values.reshape(tokens // block, block, channels),
        windows,
    )


def solution(mesh):
    return jax.shard_map(
        body,
        mesh=mesh,
        in_specs=(
            P(("seq", "head"), None),
            P(("seq", "head"), None),
            P(("seq", "head"), None),
            P("seq", None),
        ),
        out_specs=P(("seq", "head"), None),
        check_vma=False,
    )
```
